32 devices in a mesh: row: 4 (over y, core), col: 8 (over z, x).
Axes of the slice: x: 2, y: 2, z: 4, core: 2. Of those that a mesh axis runs over, the one named last changes fastest.
Arguments:
- queries: bfloat16 [8, 8, 128, 2048], P('row', 'col'), may hold values from -70 to 70
- fine_keys: bfloat16 [8, 8, 128, 2048], P('row', 'col'), may hold values from -4 to 4
- fine_values: bfloat16 [8, 8, 128, 2048], P('row', 'col'), may hold values from -6 to 6
- keep_flags: int32 [8, 8, 9], P('row', 'col'), may hold values 0 or 1
- coarse_keys: bfloat16 [1024, 2048], P('col'), may hold values from -6 to 6
- coarse_values: bfloat16 [1024, 2048], P('col'), may hold values from -6 to 6
Outputs:
- attended: bfloat16 [8, 8, 128, 2048], P('row', 'col')
The draws below stay inside these ranges and needn't reach their ends.
All inputs are finite; a program needn't handle non-finite values. No bound on the sum of `keep_flags` on one device may be relied on, other than what follows from the above.
Results may differ from the reference program's by a relative error of at most 0.0035.
Values may be sent and summed in bfloat16 or wider, within the bound.
No kernel may reach another device: no remote copies, remote signals or barrier semaphores. Data moves between devices by JAX's collectives and lax.ppermute only.
A program may use at most 128 MiB of HBM per device.

```python
import jax
import jax.numpy as jnp
from jax import lax

D = 2048
HEADS = 16
HEAD_DIM = 128
TILE = 128
NTR = 8
NTC = 8
COARSE = 1024


def drawn_pair(key):
    shape = (NTR, NTC, TILE, D)
    keys = jax.random.truncated_normal(jax.random.fold_in(key, 11), -4.0, 4.0, shape, jnp.float32)
    queries = 2.0 * jax.random.truncated_normal(jax.random.fold_in(key, 12), -4.0, 4.0, shape, jnp.float32)
    return (queries, keys)


def draw_queries(key, part):
    return drawn_pair(key)[0].astype(jnp.bfloat16)


def draw_fine_keys(key, part):
    return drawn_pair(key)[1].astype(jnp.bfloat16)


def plant(values, rng, low, top_value):
    longest = values.shape.index(max(values.shape))
    spots = []
    for shift in (0, 1):
        where = [jax.random.randint(jax.random.fold_in(rng, axis), (), 0, length) for axis, length in enumerate(values.shape)]
        where[longest] = (where[longest] + shift) % values.shape[longest]
        spots.append(tuple(where))
    return values.at[spots[0]].set(low).at[spots[1]].set(top_value)


def steps_of(key, dims, shards, low, top_value):
    def one(dim, blocks):
        draws = jax.random.uniform(jax.random.fold_in(jax.random.fold_in(key, 6), dim), (blocks,), jnp.float32, low / len(shards), top_value / len(shards))
        return jnp.repeat(jnp.exp(draws), dims[dim] // blocks).reshape((-1,) + (1,) * (len(dims) - dim - 1))

    factor_of = one(*shards[0])
    for cut in shards[1:]:
        factor_of = factor_of * one(*cut)
    return factor_of


def centred(key, shape, width, most, cuts=(), held_as=jnp.bfloat16):
    gain = steps_of(key, shape, cuts, -0.22, 0.18) if cuts else 1.0
    result = jax.random.normal(key, shape, jnp.float32) * width * gain
    return jnp.minimum(jnp.maximum(result, -most), most).astype(held_as)


def setup_inputs(seed: int = 0) -> dict:
    streams_of = jax.random.split(jax.random.key(seed), 7)
    queries = draw_queries(jax.random.fold_in(streams_of[6], 71), 0)
    fine_keys = draw_fine_keys(jax.random.fold_in(streams_of[6], 71), 0)
    fine_values = centred(streams_of[2], (NTR, NTC, TILE, D), 1.0, 6.0, ((0, 4), (1, 8)))
    keep_flags = plant((jax.random.randint(streams_of[3], (NTR, NTC, 9), 0, 3) < 2).astype(jnp.int32), jax.random.fold_in(streams_of[3], 1), 0, 1)
    coarse_keys = centred(streams_of[4], (COARSE, D), 1.0, 6.0, ((0, 8),))
    coarse_values = centred(streams_of[5], (COARSE, D), 1.0, 6.0, ((0, 8),))
    return dict(queries=queries, fine_keys=fine_keys, fine_values=fine_values, keep_flags=keep_flags, coarse_keys=coarse_keys, coarse_values=coarse_values)


def reference(queries, fine_keys, fine_values, keep_flags, coarse_keys, coarse_values):
    rows_total, cols_total, tile_len, model_width = queries.shape
    scale = HEAD_DIM ** -0.5
    stacked = jnp.stack((fine_keys, fine_values), 0)
    padded = jnp.pad(stacked, ((0, 0), (1, 1), (1, 1), (0, 0), (0, 0)))
    far_keys = coarse_keys.astype(jnp.float32).reshape(-1, HEADS, HEAD_DIM)
    far_values = coarse_values.astype(jnp.float32).reshape(-1, HEADS, HEAD_DIM)
    col_index = jnp.arange(cols_total)

    def one_row(row_at):
        band = lax.dynamic_slice_in_dim(padded, row_at, 3, 1)
        flag_row = lax.dynamic_index_in_dim(keep_flags, row_at, 0, False)
        pieces = []
        usable = []
        for row_step in range(3):
            for col_step in range(3):
                pieces.append(band[:, row_step, col_step:col_step + cols_total])
                grid_row = row_at + row_step - 1
                grid_col = col_index + col_step - 1
                inside = (grid_row >= 0) & (grid_row < rows_total) & (grid_col >= 0) & (grid_col < cols_total)
                kept_here = (flag_row[:, row_step * 3 + col_step] > 0) | (row_step == 1 and col_step == 1)
                usable.append(inside & kept_here)
        window = jnp.concatenate(pieces, axis=2).astype(jnp.float32)
        window_ok = jnp.repeat(jnp.stack(usable, 1), tile_len, axis=1)
        near_keys = window[0].reshape(cols_total, 9 * tile_len, HEADS, HEAD_DIM)
        near_values = window[1].reshape(cols_total, 9 * tile_len, HEADS, HEAD_DIM)
        query_row = lax.dynamic_index_in_dim(queries, row_at, 0, False).astype(jnp.float32)
        query_row = query_row.reshape(cols_total, tile_len, HEADS, HEAD_DIM)
        near_scores = jnp.einsum('tqhd,tkhd->thqk', query_row, near_keys) * scale
        near_scores = jnp.where(window_ok[:, None, None, :], near_scores, -jnp.inf)
        far_scores = jnp.einsum('tqhd,khd->thqk', query_row, far_keys) * scale
        largest = jnp.maximum(jnp.max(near_scores, -1), jnp.max(far_scores, -1))[..., None]
        near_probs = jnp.exp(near_scores - largest)
        far_probs = jnp.exp(far_scores - largest)
        total = jnp.sum(near_probs, -1) + jnp.sum(far_probs, -1)
        near_round = lax.optimization_barrier(near_probs.astype(jnp.bfloat16)).astype(jnp.float32)
        far_round = lax.optimization_barrier(far_probs.astype(jnp.bfloat16)).astype(jnp.float32)
        mixed = jnp.einsum('thqk,tkhd->tqhd', near_round, near_values)
        mixed = mixed + jnp.einsum('thqk,khd->tqhd', far_round, far_values)
        mixed = mixed / jnp.transpose(total, (0, 2, 1))[..., None]
        return mixed.reshape(cols_total, tile_len, model_width).astype(jnp.bfloat16)

    return lax.map(one_row, jnp.arange(rows_total))
```

```python
import functools

import jax
import jax.numpy as jnp
from jax import lax
from jax.experimental import pallas as pl
from jax.experimental.pallas import tpu as pltpu
from jax.sharding import PartitionSpec as P

HEADS = 16
HEAD_DIM = 128
LOG2_SCALE = HEAD_DIM ** (-0.5) * 1.4426950408889634


def attend(
    pad,
    ok_ref,
    q_ref,
    own_ref,
    left_ref,
    right_ref,
    far_ref,
    out_ref,
):
    bands = q_ref.shape[1]
    rows_in_band = q_ref.shape[2]
    rows = bands * rows_in_band
    key_rows = own_ref.shape[1] * rows_in_band
    tile = q_ref.shape[3]

    def one_row(i, carry):
        band, sub = i // rows_in_band, i % rows_in_band
        q0 = q_ref[0, band, sub]
        q1 = q_ref[1, band, sub]
        qq = jnp.concatenate([q0, q1], axis=0)
        nt = (((1,), (1,)), ((), ()))

        def scores(a, b):
            return lax.dot_general(a, b, nt, preferred_element_type=jnp.float32)

        far = [
            scores(qq, far_ref[c, 0]) for c in range(far_ref.shape[0])
        ]
        parts = [[], []]
        for c, s in enumerate(far):
            parts[0].append((s[:tile], None, (2, c, 0)))
            parts[1].append((s[tile:], None, (2, c, 0)))
        for a in range(3):
            j = jnp.clip(i + pad + a - 1, 0, key_rows - 1)
            kb, ks = j // rows_in_band, j % rows_in_band
            for x in range(2):
                s = scores(qq, own_ref[x, kb, 0, ks])
                for xq in range(2):
                    flag = ok_ref[(i * 2 + xq) * 9 + a * 3 + 1 + x - xq]
                    parts[xq].append((s[xq * tile : (xq + 1) * tile], flag, (x, kb, ks)))
            s = scores(q0, left_ref[kb, 0, ks])
            parts[0].append((s, ok_ref[(i * 2 + 0) * 9 + a * 3], (3, kb, ks)))
            s = scores(q1, right_ref[kb, 0, ks])
            parts[1].append((s, ok_ref[(i * 2 + 1) * 9 + a * 3 + 2], (4, kb, ks)))
        for xq in range(2):
            tiles = [
                s if flag is None else jnp.where(flag > 0, s, -jnp.inf)
                for s, flag, _ in parts[xq]
            ]
            biggest = functools.reduce(jnp.maximum, tiles)
            m = jnp.max(biggest, axis=1, keepdims=True)
            total = None
            acc = None
            for s, (_, _, (kind, u, w)) in zip(tiles, parts[xq]):
                p = jnp.exp2((s - m) * LOG2_SCALE)
                total = p if total is None else total + p
                if kind == 2:
                    v = far_ref[u, 1]
                elif kind == 3:
                    v = left_ref[u, 1, w]
                elif kind == 4:
                    v = right_ref[u, 1, w]
                else:
                    v = own_ref[kind, u, 1, w]
                o = jnp.dot(p.astype(jnp.bfloat16), v, preferred_element_type=jnp.float32)
                acc = o if acc is None else acc + o
            total = jnp.sum(total, axis=1, keepdims=True)
            out_ref[xq, band, sub] = (acc / total).astype(out_ref.dtype)
        return carry

    lax.fori_loop(0, rows, one_row, 0)


def attention(ok, q, own, left, right, far, pad):
    heads = q.shape[-1] // HEAD_DIM

    def spec(a):
        lead = a.shape[:-1]
        return pl.BlockSpec(lead + (HEAD_DIM,), lambda h, s, n=len(lead): (0,) * n + (h,))

    flops = 4 * 2 * q.shape[1] * q.shape[2] * 128 * 128 * 17 * 128 * heads
    return pl.pallas_call(
        functools.partial(attend, pad),
        grid_spec=pltpu.PrefetchScalarGridSpec(
            num_scalar_prefetch=1,
            grid=(heads,),
            in_specs=[spec(a) for a in (q, own, left, right, far)],
            out_specs=spec(q),
        ),
        out_shape=jax.ShapeDtypeStruct(q.shape, q.dtype),
        compiler_params=pltpu.CompilerParams(vmem_limit_bytes=56 * 1024 * 1024),
        cost_estimate=pl.CostEstimate(
            flops=flops, bytes_accessed=8 * 1024 * 1024, transcendentals=flops // 512
        ),
        name="attend",
    )(ok, q, own, left, right, far)


def moves(count, step):
    return [(i, i + step) for i in range(count) if 0 <= i + step < count]


def body(queries, fine_keys, fine_values, keep_flags, coarse_keys, coarse_values):
    rows_tiles, _, tile, width = queries.shape
    nrow, ncol = lax.axis_size("row"), lax.axis_size("col")
    band = min(4, nrow)
    planes = ncol // 2
    parts = band * 2
    part = width // parts
    row_at, col_at = lax.axis_index("row"), lax.axis_index("col")
    axes = ("row", "col")
    groups = [
        [(g * band + r) * ncol + 2 * z + x for x in range(2) for r in range(band)]
        for g in range(nrow // band)
        for z in range(planes)
    ]

    def by_part(a):
        return jnp.moveaxis(a.reshape(a.shape[:-1] + (parts, part)), -2, 0)

    def exchange(a):
        return lax.all_to_all(a, axes, 0, 0, axis_index_groups=groups, tiled=True)

    kv = jnp.stack([by_part(fine_keys[:, 0]), by_part(fine_values[:, 0])], 1)
    own = exchange(kv).reshape(2, band, 2, rows_tiles, tile, part)
    q = exchange(by_part(queries[:, 0])).reshape(2, band, rows_tiles, tile, part)
    flags = lax.all_gather(keep_flags, axes, axis=0, axis_index_groups=groups)
    flags = flags.reshape(2, band * rows_tiles, 9)

    left = lax.ppermute(own[1], "col", moves(ncol, 2))
    right = lax.ppermute(own[0], "col", moves(ncol, -2))

    mine = jnp.stack([by_part(coarse_keys), by_part(coarse_values)], 1)
    mine = mine.reshape((2, band) + mine.shape[1:])
    mine = lax.dynamic_index_in_dim(mine, row_at % band, 1, keepdims=False)
    far = jnp.concatenate([mine] * planes, 0)
    far = lax.all_to_all(far, "col", 0, 0, tiled=True)

    pad = 0
    if nrow > band:
        pad = 1

        def widen(a):
            line = jnp.moveaxis(a, 1, 0)
            line = line.reshape((2, band * rows_tiles) + line.shape[3:])
            above = lax.ppermute(line[:, -1:], "row", moves(nrow, band))
            below = lax.ppermute(line[:, :1], "row", moves(nrow, -band))
            extra = [line[:, :1]] * ((-2) % rows_tiles)
            line = jnp.concatenate([above, line, below] + extra, 1)
            line = line.reshape((2, -1, rows_tiles) + line.shape[2:])
            return jnp.moveaxis(line, 0, 1)

        own = jnp.stack([widen(own[0]), widen(own[1])])
        left, right = widen(left), widen(right)

    rows = jnp.arange(band * rows_tiles)[None, :, None] + (row_at // band) * band * rows_tiles
    cols = jnp.arange(2)[:, None, None] + (col_at // 2) * 2
    step = jnp.arange(9)[None, None, :]
    key_rows = rows + step // 3 - 1
    key_cols = cols + step % 3 - 1
    inside = (
        (key_rows >= 0)
        & (key_rows < rows_tiles * nrow)
        & (key_cols >= 0)
        & (key_cols < ncol)
    )
    ok = (inside & ((flags > 0) | (step == 4))).astype(jnp.int32)
    ok = jnp.moveaxis(ok, 0, 1).reshape(-1)

    out = attention(ok, q, own, left, right, far, pad)
    out = exchange(out.reshape((parts, rows_tiles, tile, part)))
    return jnp.moveaxis(out, 0, -2).reshape(queries.shape)


def solution(mesh):
    placed = (
        P("row", "col", None, None),
        P("row", "col", None, None),
        P("row", "col", None, None),
        P("row", "col", None),
        P("col", None),
        P("col", None),
    )
    return jax.shard_map(
        body, mesh=mesh, in_specs=placed, out_specs=P("row", "col", None, None), check_vma=False
    )
```

```python
import functools

import jax
import jax.numpy as jnp
from jax import lax
from jax.experimental import pallas as pl
from jax.experimental.pallas import tpu as pltpu
from jax.sharding import PartitionSpec as P

HEADS = 16
HEAD_DIM = 128
LOG2_SCALE = HEAD_DIM ** (-0.5) * 1.4426950408889634


NT = (((1,), (1,)), ((), ()))


def scores(a, b):
    return lax.dot_general(a, b, NT, preferred_element_type=jnp.float32)


def softmax_terms(pieces, flags, m):
    tiles = [
        s if flag is None else jnp.where(flag > 0, s, -jnp.inf) for s, flag in zip(pieces, flags)
    ]
    top = jnp.max(functools.reduce(jnp.maximum, tiles), axis=1, keepdims=True)
    m = top if m is None else jnp.maximum(m, top)
    powers, total = [], None
    for s in tiles:
        p = jnp.exp2((s - m) * LOG2_SCALE)
        total = p if total is None else total + p
        powers.append(p.astype(jnp.bfloat16))
    return m, jnp.sum(total, axis=1, keepdims=True), powers


def key_rows_of(i, pad, key_rows, rows_in_band):
    rows = [(a, i + pad + a - 1) for a in range(3)]
    return [(a, j // rows_in_band, j % rows_in_band) for a, j in rows if 0 <= j < key_rows]


def attend_near(pad, planes, ok_ref, q_ref, own_ref, *refs):
    far_refs, (acc_ref, stat_ref) = refs[:planes], refs[planes:]
    _, bands, rows_in_band, tile, _ = acc_ref.shape
    key_rows = own_ref.shape[1] * rows_in_band
    shards = [(f, c) for f in far_refs for c in range(2)]
    lane = lax.broadcasted_iota(jnp.int32, (tile, tile), 1)
    stat = jnp.zeros((tile, tile), jnp.float32)
    for i in range(bands * rows_in_band):
        band, sub = i // rows_in_band, i % rows_in_band
        at = key_rows_of(i, pad, key_rows, rows_in_band)
        qq = jnp.concatenate([q_ref[x, band, sub * tile : (sub + 1) * tile] for x in range(2)], 0)
        far = scores(qq, jnp.concatenate([f[c, 0] for f, c in shards], 0))
        near = scores(
            qq, jnp.concatenate([own_ref[x, kb, 0, ks] for _, kb, ks in at for x in range(2)], 0)
        )
        values = jnp.concatenate(
            [f[c, 1] for f, c in shards]
            + [own_ref[x, kb, 1, ks] for _, kb, ks in at for x in range(2)],
            0,
        )
        for xq in range(2):
            mine = slice(xq * tile, (xq + 1) * tile)
            pieces = [far[mine, n * tile : (n + 1) * tile] for n in range(len(shards))]
            pieces += [near[mine, n * tile : (n + 1) * tile] for n in range(2 * len(at))]
            flags = [None] * len(shards) + [
                ok_ref[(i * 2 + xq) * 9 + a * 3 + 1 + x - xq] for a, _, _ in at for x in range(2)
            ]
            m, total, powers = softmax_terms(pieces, flags, None)
            acc_ref[xq, band, sub] = jnp.dot(
                jnp.concatenate(powers, 1), values, preferred_element_type=jnp.float32
            )
            n = i * 2 + xq
            stat = jnp.where(lane == n, m, jnp.where(lane == n + tile // 2, total, stat))
    stat_ref[0] = stat


def attend_sides(pad, ok_ref, q_ref, left_ref, right_ref, acc_ref, stat_ref, out_ref):
    _, bands, rows_in_band, tile, _ = out_ref.shape
    rows = bands * rows_in_band
    key_rows = left_ref.shape[0] * rows_in_band
    lane = lax.broadcasted_iota(jnp.int32, (tile, tile), 1)
    stat = stat_ref[0]
    for xq, side in ((0, left_ref), (1, right_ref)):
        near_rows = [
            [i for i in range(rows) if abs(i + pad - j) <= 1] for j in range(key_rows)
        ]
        near_rows = {j: found for j, found in enumerate(near_rows) if found}
        pieces = {}
        for j, found in near_rows.items():
            qs = [
                q_ref[xq, i // rows_in_band, i % rows_in_band * tile : (i % rows_in_band + 1) * tile]
                for i in found
            ]
            s = scores(jnp.concatenate(qs, 0), side[j // rows_in_band, 0, j % rows_in_band])
            for u, i in enumerate(found):
                pieces[i, j] = s[u * tile : (u + 1) * tile]
        shrinks, totals = {}, {}
        for i in range(rows):
            n = i * 2 + xq
            m_near = jnp.max(jnp.where(lane == n, stat, -jnp.inf), axis=1, keepdims=True)
            near = jnp.max(jnp.where(lane == n + tile // 2, stat, -jnp.inf), axis=1, keepdims=True)
            at = [j for j in near_rows if (i, j) in pieces]
            flags = [ok_ref[n * 9 + (j - i - pad + 1) * 3 + 2 * xq] for j in at]
            m, total, powers = softmax_terms([pieces[i, j] for j in at], flags, m_near)
            for u, j in enumerate(at):
                pieces[i, j] = powers[u]
            shrinks[i] = jnp.exp2((m_near - m) * LOG2_SCALE)
            totals[i] = total + near * shrinks[i]
        more = {}
        for j, found in near_rows.items():
            o = jnp.dot(
                jnp.concatenate([pieces[i, j] for i in found], 0),
                side[j // rows_in_band, 1, j % rows_in_band],
                preferred_element_type=jnp.float32,
            )
            for u, i in enumerate(found):
                o_i = o[u * tile : (u + 1) * tile]
                more[i] = more[i] + o_i if i in more else o_i
        for i in range(rows):
            band, sub = i // rows_in_band, i % rows_in_band
            out = (acc_ref[xq, band, sub] * shrinks[i] + more[i]) / totals[i]
            out_ref[xq, band, sub] = out.astype(out_ref.dtype)


def by_head(a):
    lead = a.shape[:-1]
    return pl.BlockSpec(lead + (HEAD_DIM,), lambda h, s, n=len(lead): (0,) * n + (h,))


def call(kernel, name, ok, operands, in_specs, out_shape, out_specs, heads, tiles):
    flops = 4 * tiles * heads * 128 * 128 * HEAD_DIM
    return pl.pallas_call(
        kernel,
        grid_spec=pltpu.PrefetchScalarGridSpec(
            num_scalar_prefetch=1,
            grid=(heads,),
            in_specs=in_specs,
            out_specs=out_specs,
        ),
        out_shape=out_shape,
        compiler_params=pltpu.CompilerParams(vmem_limit_bytes=56 * 1024 * 1024),
        cost_estimate=pl.CostEstimate(
            flops=flops, bytes_accessed=8 * 1024 * 1024, transcendentals=flops // 512
        ),
        name=name,
    )(ok, *operands)


def near_part(ok, q, own, far, pad, shape):
    heads, tile = shape[-1] // HEAD_DIM, shape[-2]
    acc = jax.ShapeDtypeStruct(shape, jnp.float32)
    stat = jax.ShapeDtypeStruct((heads, tile, tile), jnp.float32)
    stat_spec = pl.BlockSpec((1, tile, tile), lambda h, s: (h, 0, 0))
    operands = (q, own, *far)
    tiles = shape[0] * shape[1] * shape[2] * (6 + 2 * len(far))
    return call(
        functools.partial(attend_near, pad, len(far)), "attend_near", ok, operands,
        [by_head(a) for a in operands], (acc, stat), (by_head(acc), stat_spec), heads, tiles,
    )


def side_part(ok, q, left, right, acc, stat, pad):
    heads, tile = acc.shape[-1] // HEAD_DIM, acc.shape[-2]
    out = jax.ShapeDtypeStruct(acc.shape, q.dtype)
    stat_spec = pl.BlockSpec((1, tile, tile), lambda h, s: (h, 0, 0))
    operands = (q, left, right, acc)
    tiles = acc.shape[0] * acc.shape[1] * acc.shape[2] * 3
    return call(
        functools.partial(attend_sides, pad), "attend_sides", ok, (*operands, stat),
        [by_head(a) for a in operands] + [stat_spec], out, by_head(out), heads, tiles,
    )


def moves(count, step):
    return [(i, i + step) for i in range(count) if 0 <= i + step < count]


def body(queries, fine_keys, fine_values, keep_flags, coarse_keys, coarse_values):
    rows_tiles, _, tile, width = queries.shape
    nrow, ncol = lax.axis_size("row"), lax.axis_size("col")
    band = min(4, nrow)
    planes = ncol // 2
    parts = band * 2
    part = width // parts
    row_at, col_at = lax.axis_index("row"), lax.axis_index("col")
    axes = ("row", "col")
    groups = [
        [(g * band + r) * ncol + 2 * z + x for x in range(2) for r in range(band)]
        for g in range(nrow // band)
        for z in range(planes)
    ]

    def by_part(a):
        return jnp.moveaxis(a.reshape(a.shape[:-1] + (parts, part)), -2, 0)

    def exchange(a):
        return lax.all_to_all(a, axes, 0, 0, axis_index_groups=groups, tiled=True)

    mine = jnp.stack([by_part(coarse_keys), by_part(coarse_values)], 1)
    mine = mine.reshape((2, band) + mine.shape[1:])
    mine = lax.dynamic_index_in_dim(mine, row_at % band, 1, keepdims=False)
    here = lax.dynamic_index_in_dim(mine, col_at % 2, 0, keepdims=False)
    away = lax.dynamic_index_in_dim(mine, 1 - col_at % 2, 0, keepdims=False)
    there = lax.ppermute(away, "col", [(c, c ^ 1) for c in range(ncol)])
    kv = jnp.stack([by_part(fine_keys[:, 0]), by_part(fine_values[:, 0])], 1)
    kv, there = lax.optimization_barrier((kv, there))
    own = exchange(kv)
    pair = jnp.stack([here, there])
    far = [pair] + [
        lax.ppermute(pair, "col", [(c, (c + 2 * d) % ncol) for c in range(ncol)])
        for d in range(1, planes)
    ]
    count = rows_tiles * 9
    notes = jnp.pad(keep_flags.astype(jnp.bfloat16).reshape(1, count), ((0, 15), (0, part - count)))
    queries_out = jnp.concatenate(
        [
            by_part(queries.reshape(rows_tiles * tile, width)),
            jnp.broadcast_to(notes, (parts, 16, part)),
        ],
        1,
    )
    queries_out, own, *far = lax.optimization_barrier((queries_out, own, *far))
    q = exchange(queries_out)
    flags = q[:, rows_tiles * tile, :count].reshape(2, band * rows_tiles, 9)
    q = q.reshape(2, band, rows_tiles * tile + 16, part)
    own = own.reshape(2, band, 2, rows_tiles, tile, part)

    left = lax.ppermute(own[1], "col", moves(ncol, 2))
    right = lax.ppermute(own[0], "col", moves(ncol, -2))

    pad = 0
    if nrow > band:
        pad = 1

        def widen(a):
            line = jnp.moveaxis(a, 1, 0)
            line = line.reshape((2, band * rows_tiles) + line.shape[3:])
            above = lax.ppermute(line[:, -1:], "row", moves(nrow, band))
            below = lax.ppermute(line[:, :1], "row", moves(nrow, -band))
            extra = [line[:, :1]] * ((-2) % rows_tiles)
            line = jnp.concatenate([above, line, below] + extra, 1)
            line = line.reshape((2, -1, rows_tiles) + line.shape[2:])
            return jnp.moveaxis(line, 0, 1)

        own = jnp.stack([widen(own[0]), widen(own[1])])
        left, right = widen(left), widen(right)

    rows = jnp.arange(band * rows_tiles)[None, :, None] + (row_at // band) * band * rows_tiles
    cols = jnp.arange(2)[:, None, None] + (col_at // 2) * 2
    step = jnp.arange(9)[None, None, :]
    key_rows = rows + step // 3 - 1
    key_cols = cols + step % 3 - 1
    inside = (
        (key_rows >= 0)
        & (key_rows < rows_tiles * nrow)
        & (key_cols >= 0)
        & (key_cols < ncol)
    )
    ok = (inside & ((flags > 0) | (step == 4))).astype(jnp.int32)
    ok = jnp.moveaxis(ok, 0, 1).reshape(-1)

    shape = (2, band, rows_tiles, tile, part)
    acc, stat = near_part(ok, q, own, far, pad, shape)
    out = side_part(ok, q, left, right, acc, stat, pad)
    out = exchange(out.reshape((parts, rows_tiles, tile, part)))
    return jnp.moveaxis(out, 0, -2).reshape(queries.shape)


def solution(mesh):
    placed = (
        P("row", "col", None, None),
        P("row", "col", None, None),
        P("row", "col", None, None),
        P("row", "col", None),
        P("col", None),
        P("col", None),
    )
    return jax.shard_map(
        body, mesh=mesh, in_specs=placed, out_specs=P("row", "col", None, None), check_vma=False
    )
```

```python
import functools

import jax
import jax.numpy as jnp
from jax import lax
from jax.experimental import pallas as pl
from jax.experimental.pallas import tpu as pltpu
from jax.sharding import PartitionSpec as P

HEADS = 16
HEAD_DIM = 128
LOG2_SCALE = HEAD_DIM ** (-0.5) * 1.4426950408889634


NT = (((1,), (1,)), ((), ()))
NOTE_ROWS = 32


def scores(a, b):
    return lax.dot_general(a, b, NT, preferred_element_type=jnp.float32)


def softmax_terms(pieces, masks, m):
    tiles = [s if ok is None else jnp.where(ok, s, -jnp.inf) for s, ok in zip(pieces, masks)]
    top = jnp.max(functools.reduce(jnp.maximum, tiles), axis=1, keepdims=True)
    m = top if m is None else jnp.maximum(m, top)
    powers, total = [], None
    for s in tiles:
        p = jnp.exp2((s - m) * LOG2_SCALE)
        total = p if total is None else total + p
        powers.append(p.astype(jnp.bfloat16))
    return m, jnp.sum(total, axis=1, keepdims=True), powers


def at_head(ref, h):
    return ref.at[..., h * HEAD_DIM : (h + 1) * HEAD_DIM]


class Band:
    def __init__(self, first, second, rows_in_band, tile):
        self.first, self.second, self.rows, self.tile = first, second, rows_in_band, tile
        self.cut = rows_in_band // 2

    def at(self, ref, band, n):
        return ref[band, n * self.tile : (n + 1) * self.tile]

    def key(self, band, sub):
        return self.at(self.first, band, sub)

    def value(self, band, sub):
        if sub < self.cut:
            return self.at(self.first, band, self.rows + sub)
        return self.at(self.second, band, sub - self.cut)

    def query(self, band, sub):
        return self.at(self.second, band, self.rows - self.cut + sub)

    def notes(self, band):
        start = (2 * self.rows - self.cut) * self.tile
        return self.second[band, start : start + NOTE_ROWS].astype(jnp.float32)


def attend_near(pad, rows_in_band, q_all, own_all, own_rest, *refs):
    far_all, acc_ref, stat_ref = refs[:-2], refs[-2], refs[-1]
    heads, _, rows, tile, _ = acc_ref.shape
    key_rows = own_all.shape[1] * rows_in_band
    lane = lax.broadcasted_iota(jnp.int32, (tile, tile), 1)
    for h in range(heads):
        own, qs_of = [
            [
                Band(at_head(first, h).at[x], at_head(second, h).at[x], rows_in_band, tile)
                for x in range(2)
            ]
            for first, second in ((own_all, own_rest), (own_all, q_all))
        ]
        shards = [at_head(f, h).at[c] for f in far_all for c in range(2)]
        stat = jnp.zeros((tile, tile), jnp.float32)
        for first in range(0, rows, rows_in_band):
            band = first // rows_in_band
            tiles = [(sub, x) for sub in range(rows_in_band) for x in range(2)]
            qs = [qs_of[x].query(band, sub) for sub, x in tiles]
            far = scores(jnp.concatenate(qs, 0), jnp.concatenate([f[0] for f in shards], 0))
            far_powers, near_sums = [], []
            for sub in range(rows_in_band):
                i = first + sub
                at = [(a, i + pad + a - 1) for a in range(3)]
                at = [(a, j // rows_in_band, j % rows_in_band) for a, j in at if 0 <= j < key_rows]
                window = [(a, kb, ks, x) for a, kb, ks in at for x in range(2)]
                near = scores(
                    jnp.concatenate(qs[2 * sub : 2 * sub + 2], 0),
                    jnp.concatenate([own[x].key(kb, ks) for _, kb, ks, x in window], 0),
                )
                near_powers = []
                for xq in range(2):
                    mine = slice((2 * sub + xq) * tile, (2 * sub + xq + 1) * tile)
                    pieces = [far[mine, n * tile : (n + 1) * tile] for n in range(len(shards))]
                    mine = slice(xq * tile, (xq + 1) * tile)
                    pieces += [near[mine, n * tile : (n + 1) * tile] for n in range(len(window))]
                    notes = qs_of[xq].notes(band)
                    masks = [None] * len(shards)
                    for a, _, _, x in window:
                        n = sub * 9 + (x ^ xq) * 3 + a
                        masks.append(None if x == xq and a == 1 else notes[n : n + 1] > 0)
                    m, total, powers = softmax_terms(pieces, masks, None)
                    far_powers.append(jnp.concatenate(powers[: len(shards)], 1))
                    near_powers.append(jnp.concatenate(powers[len(shards) :], 1))
                    n = i * 2 + xq
                    stat = jnp.where(lane == n, m, jnp.where(lane == n + tile // 2, total, stat))
                near_sums.append(
                    jnp.dot(
                        jnp.concatenate(near_powers, 0),
                        jnp.concatenate([own[x].value(kb, ks) for _, kb, ks, x in window], 0),
                        preferred_element_type=jnp.float32,
                    )
                )
            sums = jnp.dot(
                jnp.concatenate(far_powers, 0),
                jnp.concatenate([f[1] for f in shards], 0),
                preferred_element_type=jnp.float32,
            ) + jnp.concatenate(near_sums, 0)
            for u, (sub, x) in enumerate(tiles):
                acc_ref[h, x, first + sub] = sums[u * tile : (u + 1) * tile]
        stat_ref[h] = stat


def attend_sides(pad, rows_in_band, q_all, *refs):
    sides, (acc_ref, stat_ref, out_ref) = refs[:4], refs[4:]
    heads, _, rows, tile, _ = acc_ref.shape
    key_rows = sides[0].shape[0] * rows_in_band
    lane = lax.broadcasted_iota(jnp.int32, (tile, tile), 1)
    near_rows = [[i for i in range(rows) if abs(i + pad - j) <= 1] for j in range(key_rows)]
    near_rows = {j: found for j, found in enumerate(near_rows) if found}
    for h, xq in [(h, xq) for h in range(heads) for xq in range(2)]:
        stat = stat_ref[h]
        first, second = [at_head(a, h) for a in sides[2 * xq : 2 * xq + 2]]
        side = Band(first, second, rows_in_band, tile)
        mine = Band(None, at_head(q_all, h).at[xq], rows_in_band, tile)
        pieces = {}
        for j, found in near_rows.items():
            qs = [mine.query(i // rows_in_band, i % rows_in_band) for i in found]
            s = scores(jnp.concatenate(qs, 0), side.key(j // rows_in_band, j % rows_in_band))
            for u, i in enumerate(found):
                pieces[i, j] = s[u * tile : (u + 1) * tile]
        shrinks, totals = {}, {}
        for i in range(rows):
            n = i * 2 + xq
            m_near = jnp.max(jnp.where(lane == n, stat, -jnp.inf), axis=1, keepdims=True)
            near = jnp.max(jnp.where(lane == n + tile // 2, stat, -jnp.inf), axis=1, keepdims=True)
            at = [j for j in near_rows if (i, j) in pieces]
            notes = mine.notes(i // rows_in_band)
            masks = []
            for j in at:
                n = i % rows_in_band * 9 + 6 + j - i - pad + 1
                masks.append(notes[n : n + 1] > 0)
            m, total, powers = softmax_terms([pieces[i, j] for j in at], masks, m_near)
            for u, j in enumerate(at):
                pieces[i, j] = powers[u]
            shrinks[i] = jnp.exp2((m_near - m) * LOG2_SCALE)
            totals[i] = total + near * shrinks[i]
        more = {}
        for j, found in near_rows.items():
            o = jnp.dot(
                jnp.concatenate([pieces[i, j] for i in found], 0),
                side.value(j // rows_in_band, j % rows_in_band),
                preferred_element_type=jnp.float32,
            )
            for u, i in enumerate(found):
                o_i = o[u * tile : (u + 1) * tile]
                more[i] = more[i] + o_i if i in more else o_i
        for i in range(rows):
            out = (acc_ref[h, xq, i] * shrinks[i] + more[i]) / totals[i]
            band, start = i // rows_in_band, i % rows_in_band * tile
            out_ref[xq, band, start : start + tile, h * HEAD_DIM : (h + 1) * HEAD_DIM] = out.astype(
                out_ref.dtype
            )


VMEM = pl.BlockSpec(memory_space=pltpu.VMEM)


def call(kernel, name, operands, out_shape, tiles):
    flops = 4 * tiles * 128 * 128 * HEAD_DIM
    return pl.pallas_call(
        kernel,
        in_specs=[VMEM] * len(operands),
        out_specs=jax.tree.map(lambda _: VMEM, out_shape),
        out_shape=out_shape,
        compiler_params=pltpu.CompilerParams(vmem_limit_bytes=40 * 1024 * 1024),
        cost_estimate=pl.CostEstimate(
            flops=flops, bytes_accessed=4 * 1024 * 1024, transcendentals=flops // 512
        ),
        name=name,
    )(*operands)


def start_pack(pieces, out_ref, sem):
    part, copies, at = out_ref.shape[-1], [], 0
    for n, (ref, first, end) in enumerate(pieces):
        for p in range(out_ref.shape[0]):
            copies.append(
                pltpu.make_async_copy(
                    ref.at[first:end, p * part : (p + 1) * part],
                    out_ref.at[p, at : at + end - first],
                    sem.at[n * out_ref.shape[0] + p],
                )
            )
        at += end - first
    for copy in copies:
        copy.start()
    return copies, at


def pack_first(cut, k_ref, v_ref, out_ref, sem):
    for copy in start_pack(((k_ref, 0, k_ref.shape[0]), (v_ref, 0, cut)), out_ref, sem)[0]:
        copy.wait()


def pack_second(cut, row_size, col_size, flags_ref, v_ref, q_ref, out_ref, sem):
    rows = q_ref.shape[0]
    copies, at = start_pack(((v_ref, cut, rows), (q_ref, 0, rows)), out_ref, sem)
    row_at, col_at = lax.axis_index("row"), lax.axis_index("col")
    tiles = flags_ref.shape[0]
    line = lax.broadcasted_iota(jnp.int32, (NOTE_ROWS, out_ref.shape[-1]), 0)
    notes = jnp.zeros(line.shape, jnp.float32)
    inner = 1 - 2 * (col_at % 2)
    for t in range(tiles):
        for kind, b in enumerate((0, inner, -inner)):
            for a in range(3):
                row, col = row_at * tiles + t + a - 1, col_at + b
                ok = (row >= 0) & (row < row_size * tiles) & (col >= 0) & (col < col_size)
                if kind or a != 1:
                    ok = ok & (flags_ref[t, 0, a * 3 + 1 + b] > 0)
                notes = jnp.where(line == t * 9 + kind * 3 + a, jnp.where(ok, 1.0, 0.0), notes)
    notes = notes.astype(out_ref.dtype)
    for p in range(out_ref.shape[0]):
        out_ref[p, at:] = notes
    for copy in copies:
        copy.wait()


def packed(kernel, name, small, arrays, parts, rows):
    width = arrays[0].shape[1]
    return pl.pallas_call(
        kernel,
        in_specs=[pl.BlockSpec(memory_space=pltpu.SMEM)] * len(small)
        + [pl.BlockSpec(memory_space=pltpu.HBM)] * len(arrays),
        out_specs=VMEM,
        out_shape=jax.ShapeDtypeStruct(
            (parts, rows, width // parts), arrays[0].dtype
        ),
        scratch_shapes=[pltpu.SemaphoreType.DMA((len(arrays) * parts,))],
        compiler_params=pltpu.CompilerParams(vmem_limit_bytes=60 * 1024 * 1024),
        cost_estimate=pl.CostEstimate(flops=0, bytes_accessed=3 * 1024 * 1024, transcendentals=0),
        name=name,
    )(*small, *arrays)


def unpack(got_ref, out_ref):
    part = got_ref.shape[-1]
    for p in range(got_ref.shape[0]):
        out_ref[:, p * part : (p + 1) * part] = got_ref[p]


def moves(count, step):
    return [(i, i + step) for i in range(count) if 0 <= i + step < count]


def body(queries, fine_keys, fine_values, keep_flags, coarse_keys, coarse_values):
    rows_tiles, _, tile, width = queries.shape
    nrow, ncol = lax.axis_size("row"), lax.axis_size("col")
    band = min(4, nrow)
    planes = ncol // 2
    parts = band * 2
    part = width // parts
    rows = rows_tiles * tile
    row_at, col_at = lax.axis_index("row"), lax.axis_index("col")
    x_at, r_at = col_at % 2, row_at % band
    axes = ("row", "col")
    pad = 1 if nrow > band else 0
    groups = [
        [(g * band + r) * ncol + 2 * z + x for x in range(2) for r in range(band)]
        for g in range(nrow // band)
        for z in range(planes)
    ]

    def exchange(a):
        return lax.all_to_all(a, axes, 0, 0, axis_index_groups=groups, tiled=True)

    def coarse_of(x):
        at = (x * band + r_at) * part
        return jnp.stack(
            [lax.dynamic_slice_in_dim(c, at, part, 1) for c in (coarse_keys, coarse_values)]
        )

    here, away = coarse_of(x_at), coarse_of(1 - x_at)
    there = lax.ppermute(away, "col", [(c, c ^ 1) for c in range(ncol)])

    k, v, q = [a.reshape(rows, width) for a in (fine_keys, fine_values, queries)]
    cut = rows_tiles // 2 * tile
    sent = packed(functools.partial(pack_first, cut), "pack_first", (), (k, v), parts, rows + cut)
    sent, there = lax.optimization_barrier((sent, there))
    own = exchange(sent).reshape(2, band, rows + cut, part)
    pair = jnp.stack([here, there])
    far = [pair] + [
        lax.ppermute(pair, "col", [(c, (c + 2 * d) % ncol) for c in range(ncol)])
        for d in range(1, planes)
    ]

    def widen(a):
        line = a.reshape(band, 2, rows_tiles, tile, part)
        line = jnp.moveaxis(line, 1, 0).reshape(2, band * rows_tiles, tile, part)
        above = lax.ppermute(line[:, -1:], "row", moves(nrow, band))
        below = lax.ppermute(line[:, :1], "row", moves(nrow, -band))
        extra = [line[:, :1]] * ((-2) % rows_tiles)
        line = jnp.concatenate([above, line, below] + extra, 1)
        line = jnp.moveaxis(line.reshape(2, -1, rows_tiles, tile, part), 0, 1)
        return line.reshape(-1, 2 * rows, part)

    sent = packed(
        functools.partial(pack_second, cut, nrow, ncol),
        "pack_second",
        (keep_flags,),
        (v, q),
        parts,
        2 * rows - cut + NOTE_ROWS,
    )
    sent, far[2] = lax.optimization_barrier((sent, far[2]))
    q = exchange(sent).reshape(2, band, 2 * rows - cut + NOTE_ROWS, part)
    right_going, left_going = moves(ncol, 2), moves(ncol, -2)
    left, right = lax.ppermute(own[1], "col", right_going), lax.ppermute(own[0], "col", left_going)
    rest = q[:, :, : rows - cut]
    rest, far = lax.optimization_barrier((rest, far))
    left_rest = lax.ppermute(rest[1], "col", right_going)
    right_rest = lax.ppermute(rest[0], "col", left_going)
    own_rest = q
    if pad:

        def widened(first, second):
            both = widen(jnp.concatenate([first, second], 1))
            return both[:, : rows + cut], both[:, rows + cut :]

        left, left_rest = widened(left, left_rest)
        right, right_rest = widened(right, right_rest)
        wide = [widened(own[x], rest[x]) for x in range(2)]
        own, own_rest = jnp.stack([w[0] for w in wide]), jnp.stack([w[1] for w in wide])

    count, heads = band * rows_tiles, part // HEAD_DIM
    acc = jax.ShapeDtypeStruct((heads, 2, count, tile, HEAD_DIM), jnp.float32)
    stat = jax.ShapeDtypeStruct((heads, tile, tile), jnp.float32)
    acc, stat = call(
        functools.partial(attend_near, pad, rows_tiles),
        "attend_near",
        (q, own, own_rest, *far),
        (acc, stat),
        heads * 2 * count * (6 + 2 * planes),
    )
    out = call(
        functools.partial(attend_sides, pad, rows_tiles),
        "attend_sides",
        (q, left, left_rest, right, right_rest, acc, stat),
        jax.ShapeDtypeStruct((2, band, rows, part), queries.dtype),
        heads * 2 * count * 3,
    )
    out = exchange(out.reshape(parts, rows, part))
    out = call(unpack, "unpack", (out,), jax.ShapeDtypeStruct((rows, width), queries.dtype), 0)
    return out.reshape(queries.shape)


def solution(mesh):
    placed = (
        P("row", "col", None, None),
        P("row", "col", None, None),
        P("row", "col", None, None),
        P("row", "col", None),
        P("col", None),
        P("col", None),
    )
    return jax.shard_map(
        body, mesh=mesh, in_specs=placed, out_specs=P("row", "col", None, None), check_vma=False
    )
```

```python
import functools

import jax
import jax.numpy as jnp
from jax import lax
from jax.experimental import pallas as pl
from jax.experimental.pallas import tpu as pltpu
from jax.sharding import PartitionSpec as P

HEADS = 16
HEAD_DIM = 128
LOG2_SCALE = HEAD_DIM ** (-0.5) * 1.4426950408889634


NT = (((1,), (1,)), ((), ()))
NOTE_ROWS = 16


def scores(a, b):
    return lax.dot_general(a, b, NT, preferred_element_type=jnp.float32)


def softmax_terms(pieces, masks, m):
    tiles = [s if ok is None else jnp.where(ok, s, -jnp.inf) for s, ok in zip(pieces, masks)]
    top = jnp.max(functools.reduce(jnp.maximum, tiles), axis=1, keepdims=True)
    m = top if m is None else jnp.maximum(m, top)
    powers, total = [], None
    for s in tiles:
        p = jnp.exp2((s - m) * LOG2_SCALE)
        total = p if total is None else total + p
        powers.append(p.astype(jnp.bfloat16))
    return m, jnp.sum(total, axis=1, keepdims=True), powers


def at_head(ref, h):
    return ref.at[..., h * HEAD_DIM : (h + 1) * HEAD_DIM]


class Band:
    def __init__(self, first, second, rows_in_band, tile, whole=None):
        self.first, self.second, self.rows, self.tile = first, second, rows_in_band, tile
        self.whole = whole
        self.cut = rows_in_band // 2

    def at(self, ref, band, n):
        return ref[band, n * self.tile : (n + 1) * self.tile]

    def key(self, band, sub):
        return self.at(self.first, band, sub)

    def value(self, band, sub):
        if sub < self.cut:
            return self.at(self.first, band, self.rows + sub)
        return self.at(self.second, band, sub - self.cut)

    def query(self, band, sub):
        return self.at(self.second, band, self.rows - self.cut + sub)

    def notes(self, band, sub):
        start, lane = (2 * self.rows - self.cut) * self.tile, sub * HEAD_DIM
        notes = self.whole[band, start : start + NOTE_ROWS, lane : lane + HEAD_DIM]
        return notes.astype(jnp.float32)


def attend_near(pad, rows_in_band, q_all, own_all, own_rest, *refs):
    far_all, acc_ref, stat_ref = refs[:-2], refs[-2], refs[-1]
    heads, _, rows, tile, _ = acc_ref.shape
    key_rows = own_all.shape[1] * rows_in_band
    lane = lax.broadcasted_iota(jnp.int32, (tile, tile), 1)
    for h in range(heads):
        own, qs_of = [
            [
                Band(at_head(first, h).at[x], at_head(second, h).at[x], rows_in_band, tile, q_all.at[x])
                for x in range(2)
            ]
            for first, second in ((own_all, own_rest), (own_all, q_all))
        ]
        shards = [at_head(f, h).at[c] for f in far_all for c in range(2)]
        stat = jnp.zeros((tile, tile), jnp.float32)
        for first in range(0, rows, rows_in_band):
            band = first // rows_in_band
            tiles = [(sub, x) for sub in range(rows_in_band) for x in range(2)]
            qs = [qs_of[x].query(band, sub) for sub, x in tiles]
            far = scores(jnp.concatenate(qs, 0), jnp.concatenate([f[0] for f in shards], 0))
            far_powers, near_sums = [], []
            for sub in range(rows_in_band):
                i = first + sub
                at = [(a, i + pad + a - 1) for a in range(3)]
                at = [(a, j // rows_in_band, j % rows_in_band) for a, j in at if 0 <= j < key_rows]
                window = [(a, kb, ks, x) for a, kb, ks in at for x in range(2)]
                near = scores(
                    jnp.concatenate(qs[2 * sub : 2 * sub + 2], 0),
                    jnp.concatenate([own[x].key(kb, ks) for _, kb, ks, x in window], 0),
                )
                near_powers = []
                for xq in range(2):
                    mine = slice((2 * sub + xq) * tile, (2 * sub + xq + 1) * tile)
                    pieces = [far[mine, n * tile : (n + 1) * tile] for n in range(len(shards))]
                    mine = slice(xq * tile, (xq + 1) * tile)
                    pieces += [near[mine, n * tile : (n + 1) * tile] for n in range(len(window))]
                    notes = qs_of[xq].notes(band, sub)
                    masks = [None] * len(shards)
                    for a, _, _, x in window:
                        n = (x ^ xq) * 3 + a
                        masks.append(None if x == xq and a == 1 else notes[n : n + 1] > 0)
                    m, total, powers = softmax_terms(pieces, masks, None)
                    far_powers.append(jnp.concatenate(powers[: len(shards)], 1))
                    near_powers.append(jnp.concatenate(powers[len(shards) :], 1))
                    n = i * 2 + xq
                    stat = jnp.where(lane == n, m, jnp.where(lane == n + tile // 2, total, stat))
                near_sums.append(
                    jnp.dot(
                        jnp.concatenate(near_powers, 0),
                        jnp.concatenate([own[x].value(kb, ks) for _, kb, ks, x in window], 0),
                        preferred_element_type=jnp.float32,
                    )
                )
            sums = jnp.dot(
                jnp.concatenate(far_powers, 0),
                jnp.concatenate([f[1] for f in shards], 0),
                preferred_element_type=jnp.float32,
            ) + jnp.concatenate(near_sums, 0)
            for u, (sub, x) in enumerate(tiles):
                acc_ref[h, x, first + sub] = sums[u * tile : (u + 1) * tile]
        stat_ref[h] = stat


def attend_sides(pad, rows_in_band, q_all, *refs):
    far_sides, (acc_ref, stat_ref, out_ref), sides, sem = refs[:4], refs[4:7], refs[7:11], refs[11]
    copies = [
        pltpu.make_async_copy(source, target, sem.at[n])
        for n, (source, target) in enumerate(zip(far_sides, sides))
    ]
    for copy in copies:
        copy.start()
    heads, _, rows, tile, _ = acc_ref.shape
    key_rows = sides[0].shape[0] * rows_in_band
    lane = lax.broadcasted_iota(jnp.int32, (tile, tile), 1)
    near_rows = [[i for i in range(rows) if abs(i + pad - j) <= 1] for j in range(key_rows)]
    near_rows = {j: found for j, found in enumerate(near_rows) if found}
    for h, xq in [(h, xq) for xq in range(2) for h in range(heads)]:
        if h == 0:
            copies[2 * xq].wait()
            copies[2 * xq + 1].wait()
        stat = stat_ref[h]
        first, second = [at_head(a, h) for a in sides[2 * xq : 2 * xq + 2]]
        side = Band(first, second, rows_in_band, tile)
        mine = Band(None, at_head(q_all, h).at[xq], rows_in_band, tile, q_all.at[xq])
        pieces = {}
        for j, found in near_rows.items():
            qs = [mine.query(i // rows_in_band, i % rows_in_band) for i in found]
            s = scores(jnp.concatenate(qs, 0), side.key(j // rows_in_band, j % rows_in_band))
            for u, i in enumerate(found):
                pieces[i, j] = s[u * tile : (u + 1) * tile]
        shrinks, totals = {}, {}
        for i in range(rows):
            n = i * 2 + xq
            m_near = jnp.max(jnp.where(lane == n, stat, -jnp.inf), axis=1, keepdims=True)
            near = jnp.max(jnp.where(lane == n + tile // 2, stat, -jnp.inf), axis=1, keepdims=True)
            at = [j for j in near_rows if (i, j) in pieces]
            notes = mine.notes(i // rows_in_band, i % rows_in_band)
            masks = []
            for j in at:
                n = 6 + j - i - pad + 1
                masks.append(notes[n : n + 1] > 0)
            m, total, powers = softmax_terms([pieces[i, j] for j in at], masks, m_near)
            for u, j in enumerate(at):
                pieces[i, j] = powers[u]
            shrinks[i] = jnp.exp2((m_near - m) * LOG2_SCALE)
            totals[i] = total + near * shrinks[i]
        more = {}
        for j, found in near_rows.items():
            o = jnp.dot(
                jnp.concatenate([pieces[i, j] for i in found], 0),
                side.value(j // rows_in_band, j % rows_in_band),
                preferred_element_type=jnp.float32,
            )
            for u, i in enumerate(found):
                o_i = o[u * tile : (u + 1) * tile]
                more[i] = more[i] + o_i if i in more else o_i
        for i in range(rows):
            out = (acc_ref[h, xq, i] * shrinks[i] + more[i]) / totals[i]
            band, start = i // rows_in_band, i % rows_in_band * tile
            out_ref[xq, band, start : start + tile, h * HEAD_DIM : (h + 1) * HEAD_DIM] = out.astype(
                out_ref.dtype
            )


VMEM = pl.BlockSpec(memory_space=pltpu.VMEM)


def call(kernel, name, operands, out_shape, tiles, specs=None, scratch=()):
    flops = 4 * tiles * 128 * 128 * HEAD_DIM
    return pl.pallas_call(
        kernel,
        in_specs=specs or [VMEM] * len(operands),
        out_specs=jax.tree.map(lambda _: VMEM, out_shape),
        out_shape=out_shape,
        scratch_shapes=scratch,
        compiler_params=pltpu.CompilerParams(vmem_limit_bytes=40 * 1024 * 1024),
        cost_estimate=pl.CostEstimate(
            flops=flops, bytes_accessed=4 * 1024 * 1024, transcendentals=flops // 512
        ),
        name=name,
    )(*operands)


def start_pack(pieces, out_ref, sem):
    part, copies, at = out_ref.shape[-1], [], 0
    for n, (ref, first, end) in enumerate(pieces):
        for p in range(out_ref.shape[0]):
            copies.append(
                pltpu.make_async_copy(
                    ref.at[first:end, p * part : (p + 1) * part],
                    out_ref.at[p, at : at + end - first],
                    sem.at[n * out_ref.shape[0] + p],
                )
            )
        at += end - first
    for copy in copies:
        copy.start()
    return copies, at


def pack_first(cut, k_ref, v_ref, out_ref, sem):
    for copy in start_pack(((k_ref, 0, k_ref.shape[0]), (v_ref, 0, cut)), out_ref, sem)[0]:
        copy.wait()


def pack_second(cut, row_size, col_size, flags_ref, v_ref, q_ref, out_ref, sem):
    rows = q_ref.shape[0]
    copies, at = start_pack(((v_ref, cut, rows), (q_ref, 0, rows)), out_ref, sem)
    row_at, col_at = lax.axis_index("row"), lax.axis_index("col")
    tiles = flags_ref.shape[0]
    line = lax.broadcasted_iota(jnp.int32, (NOTE_ROWS, HEAD_DIM), 0)
    blocks = []
    inner = 1 - 2 * (col_at % 2)
    for t in range(tiles):
        notes = jnp.zeros(line.shape, jnp.float32)
        for kind, b in enumerate((0, inner, -inner)):
            for a in range(3):
                row, col = row_at * tiles + t + a - 1, col_at + b
                ok = (row >= 0) & (row < row_size * tiles) & (col >= 0) & (col < col_size)
                if kind or a != 1:
                    ok = ok & (flags_ref[t, 0, a * 3 + 1 + b] > 0)
                notes = jnp.where(line == kind * 3 + a, jnp.where(ok, 1.0, 0.0), notes)
        blocks.append(notes.astype(out_ref.dtype))
    for p in range(out_ref.shape[0]):
        for t, notes in enumerate(blocks):
            out_ref[p, at:, t * HEAD_DIM : (t + 1) * HEAD_DIM] = notes
    for copy in copies:
        copy.wait()


def packed(kernel, name, small, arrays, parts, rows):
    width = arrays[0].shape[1]
    return pl.pallas_call(
        kernel,
        in_specs=[pl.BlockSpec(memory_space=pltpu.SMEM)] * len(small)
        + [pl.BlockSpec(memory_space=pltpu.HBM)] * len(arrays),
        out_specs=VMEM,
        out_shape=jax.ShapeDtypeStruct(
            (parts, rows, width // parts), arrays[0].dtype
        ),
        scratch_shapes=[pltpu.SemaphoreType.DMA((len(arrays) * parts,))],
        compiler_params=pltpu.CompilerParams(vmem_limit_bytes=60 * 1024 * 1024),
        cost_estimate=pl.CostEstimate(flops=0, bytes_accessed=3 * 1024 * 1024, transcendentals=0),
        name=name,
    )(*small, *arrays)


def unpack(got_ref, out_ref):
    part = got_ref.shape[-1]
    for p in range(got_ref.shape[0]):
        out_ref[:, p * part : (p + 1) * part] = got_ref[p]


def moves(count, step):
    return [(i, i + step) for i in range(count) if 0 <= i + step < count]


def body(queries, fine_keys, fine_values, keep_flags, coarse_keys, coarse_values):
    rows_tiles, _, tile, width = queries.shape
    nrow, ncol = lax.axis_size("row"), lax.axis_size("col")
    band = min(4, nrow)
    planes = ncol // 2
    parts = band * 2
    part = width // parts
    rows = rows_tiles * tile
    row_at, col_at = lax.axis_index("row"), lax.axis_index("col")
    x_at, r_at = col_at % 2, row_at % band
    axes = ("row", "col")
    pad = 1 if nrow > band else 0
    groups = [
        [(g * band + r) * ncol + 2 * z + x for x in range(2) for r in range(band)]
        for g in range(nrow // band)
        for z in range(planes)
    ]

    def exchange(a):
        return lax.all_to_all(a, axes, 0, 0, axis_index_groups=groups, tiled=True)

    def coarse_of(x):
        at = (x * band + r_at) * part
        return jnp.stack(
            [lax.dynamic_slice_in_dim(c, at, part, 1) for c in (coarse_keys, coarse_values)]
        )

    here, away = coarse_of(x_at), coarse_of(1 - x_at)
    there = lax.ppermute(away, "col", [(c, c ^ 1) for c in range(ncol)])

    k, v, q = [a.reshape(rows, width) for a in (fine_keys, fine_values, queries)]
    cut = rows_tiles // 2 * tile
    sent = packed(functools.partial(pack_first, cut), "pack_first", (), (k, v), parts, rows + cut)
    sent, there = lax.optimization_barrier((sent, there))
    own = exchange(sent).reshape(2, band, rows + cut, part)
    pair = jnp.stack([here, there])
    far = [pair] + [
        lax.ppermute(pair, "col", [(c, (c + 2 * d) % ncol) for c in range(ncol)])
        for d in range(1, planes)
    ]

    def widen(a):
        line = a.reshape(band, 2, rows_tiles, tile, part)
        line = jnp.moveaxis(line, 1, 0).reshape(2, band * rows_tiles, tile, part)
        above = lax.ppermute(line[:, -1:], "row", moves(nrow, band))
        below = lax.ppermute(line[:, :1], "row", moves(nrow, -band))
        extra = [line[:, :1]] * ((-2) % rows_tiles)
        line = jnp.concatenate([above, line, below] + extra, 1)
        line = jnp.moveaxis(line.reshape(2, -1, rows_tiles, tile, part), 0, 1)
        return line.reshape(-1, 2 * rows, part)

    sent = packed(
        functools.partial(pack_second, cut, nrow, ncol),
        "pack_second",
        (keep_flags,),
        (v, q),
        parts,
        2 * rows - cut + NOTE_ROWS,
    )
    sent, far[2] = lax.optimization_barrier((sent, far[2]))
    q = exchange(sent).reshape(2, band, 2 * rows - cut + NOTE_ROWS, part)
    right_going, left_going = moves(ncol, 2), moves(ncol, -2)
    left, right = lax.ppermute(own[1], "col", right_going), lax.ppermute(own[0], "col", left_going)
    rest = q[:, :, : rows - cut]
    rest, far = lax.optimization_barrier((rest, far))
    left_rest = lax.ppermute(rest[1], "col", right_going)
    right_rest = lax.ppermute(rest[0], "col", left_going)
    own_rest = q
    if pad:

        def widened(first, second):
            both = widen(jnp.concatenate([first, second], 1))
            return both[:, : rows + cut], both[:, rows + cut :]

        left, left_rest = widened(left, left_rest)
        right, right_rest = widened(right, right_rest)
        wide = [widened(own[x], rest[x]) for x in range(2)]
        own, own_rest = jnp.stack([w[0] for w in wide]), jnp.stack([w[1] for w in wide])

    count, heads = band * rows_tiles, part // HEAD_DIM
    acc = jax.ShapeDtypeStruct((heads, 2, count, tile, HEAD_DIM), jnp.float32)
    stat = jax.ShapeDtypeStruct((heads, tile, tile), jnp.float32)
    acc, stat = call(
        functools.partial(attend_near, pad, rows_tiles),
        "attend_near",
        (q, own, own_rest, *far),
        (acc, stat),
        heads * 2 * count * (6 + 2 * planes),
    )
    sides = (left, left_rest, right, right_rest)
    out = call(
        functools.partial(attend_sides, pad, rows_tiles),
        "attend_sides",
        (q, *sides, acc, stat),
        jax.ShapeDtypeStruct((2, band, rows, part), queries.dtype),
        heads * 2 * count * 3,
        [VMEM] + [pl.BlockSpec(memory_space=pl.ANY)] * 4 + [VMEM] * 2,
        [pltpu.VMEM(a.shape, a.dtype) for a in sides] + [pltpu.SemaphoreType.DMA((4,))],
    )
    out = exchange(out.reshape(parts, rows, part))
    out = call(unpack, "unpack", (out,), jax.ShapeDtypeStruct((rows, width), queries.dtype), 0)
    return out.reshape(queries.shape)


def solution(mesh):
    placed = (
        P("row", "col", None, None),
        P("row", "col", None, None),
        P("row", "col", None, None),
        P("row", "col", None),
        P("col", None),
        P("col", None),
    )
    return jax.shard_map(
        body, mesh=mesh, in_specs=placed, out_specs=P("row", "col", None, None), check_vma=False
    )
```

```python
import functools

import jax
import jax.numpy as jnp
from jax import lax
from jax.experimental import pallas as pl
from jax.experimental.pallas import tpu as pltpu
from jax.sharding import PartitionSpec as P

HEADS = 16
HEAD_DIM = 128
LOG2_SCALE = HEAD_DIM ** (-0.5) * 1.4426950408889634


NT = (((1,), (1,)), ((), ()))
NOTE_ROWS = 16


def scores(a, b):
    return lax.dot_general(a, b, NT, preferred_element_type=jnp.float32)


def softmax_terms(pieces, masks, m):
    tiles = [s if ok is None else jnp.where(ok, s, -jnp.inf) for s, ok in zip(pieces, masks)]
    top = jnp.max(functools.reduce(jnp.maximum, tiles), axis=1, keepdims=True)
    m = top if m is None else jnp.maximum(m, top)
    powers, total = [], None
    for s in tiles:
        p = jnp.exp2((s - m) * LOG2_SCALE)
        total = p if total is None else total + p
        powers.append(p.astype(jnp.bfloat16))
    return m, jnp.sum(total, axis=1, keepdims=True), powers


def at_head(ref, h):
    return ref.at[..., h * HEAD_DIM : (h + 1) * HEAD_DIM]


class Band:
    def __init__(self, first, second, rows_in_band, tile, whole=None):
        self.first, self.second, self.rows, self.tile = first, second, rows_in_band, tile
        self.whole = whole
        self.cut = rows_in_band // 2

    def at(self, ref, band, n):
        return ref[band, n * self.tile : (n + 1) * self.tile]

    def key(self, band, sub):
        return self.at(self.first, band, sub)

    def value(self, band, sub):
        if sub < self.cut:
            return self.at(self.first, band, self.rows + sub)
        return self.at(self.second, band, sub - self.cut)

    def query(self, band, sub):
        return self.at(self.second, band, self.rows - self.cut + sub)

    def notes(self, band, sub):
        start, lane = (2 * self.rows - self.cut) * self.tile, sub * HEAD_DIM
        notes = self.whole[band, start : start + NOTE_ROWS, lane : lane + HEAD_DIM]
        return notes.astype(jnp.float32)


def attend_near(pad, rows_in_band, q_all, own_all, own_rest, *refs):
    planes = len(refs) // 2 - 1
    far_out, (acc_ref, stat_ref) = refs[:planes], refs[planes : planes + 2]
    far_all, sem = refs[planes + 2 : -1], refs[-1]
    copies = [
        pltpu.make_async_copy(source, target, sem.at[n])
        for n, (source, target) in enumerate(zip(far_out, far_all))
    ]
    for copy in copies:
        copy.start()
    heads, _, rows, tile, _ = acc_ref.shape
    key_rows = own_all.shape[1] * rows_in_band
    lane = lax.broadcasted_iota(jnp.int32, (tile, tile), 1)
    for h in range(heads):
        own, qs_of = [
            [
                Band(at_head(first, h).at[x], at_head(second, h).at[x], rows_in_band, tile, q_all.at[x])
                for x in range(2)
            ]
            for first, second in ((own_all, own_rest), (own_all, q_all))
        ]
        shards = [at_head(f, h).at[c] for f in far_all for c in range(2)]
        stat = jnp.zeros((tile, tile), jnp.float32)
        for first in range(0, rows, rows_in_band):
            band = first // rows_in_band
            tiles = [(sub, x) for sub in range(rows_in_band) for x in range(2)]
            qs = [qs_of[x].query(band, sub) for sub, x in tiles]
            windows, nears = [], []
            for sub in range(rows_in_band):
                at = [(a, first + sub + pad + a - 1) for a in range(3)]
                at = [(a, j // rows_in_band, j % rows_in_band) for a, j in at if 0 <= j < key_rows]
                window = [(a, kb, ks, x) for a, kb, ks in at for x in range(2)]
                windows.append(window)
                nears.append(
                    scores(
                        jnp.concatenate(qs[2 * sub : 2 * sub + 2], 0),
                        jnp.concatenate([own[x].key(kb, ks) for _, kb, ks, x in window], 0),
                    )
                )
            if h == 0 and first == 0:
                for copy in copies:
                    copy.wait()
            far = scores(jnp.concatenate(qs, 0), jnp.concatenate([f[0] for f in shards], 0))
            far_powers, near_sums = [], []
            for sub in range(rows_in_band):
                i, window, near = first + sub, windows[sub], nears[sub]
                near_powers = []
                for xq in range(2):
                    mine = slice((2 * sub + xq) * tile, (2 * sub + xq + 1) * tile)
                    pieces = [far[mine, n * tile : (n + 1) * tile] for n in range(len(shards))]
                    mine = slice(xq * tile, (xq + 1) * tile)
                    pieces += [near[mine, n * tile : (n + 1) * tile] for n in range(len(window))]
                    notes = qs_of[xq].notes(band, sub)
                    masks = [None] * len(shards)
                    for a, _, _, x in window:
                        n = (x ^ xq) * 3 + a
                        masks.append(None if x == xq and a == 1 else notes[n : n + 1] > 0)
                    m, total, powers = softmax_terms(pieces, masks, None)
                    far_powers.append(jnp.concatenate(powers[: len(shards)], 1))
                    near_powers.append(jnp.concatenate(powers[len(shards) :], 1))
                    n = i * 2 + xq
                    stat = jnp.where(lane == n, m, jnp.where(lane == n + tile // 2, total, stat))
                near_sums.append(
                    jnp.dot(
                        jnp.concatenate(near_powers, 0),
                        jnp.concatenate([own[x].value(kb, ks) for _, kb, ks, x in window], 0),
                        preferred_element_type=jnp.float32,
                    )
                )
            sums = jnp.dot(
                jnp.concatenate(far_powers, 0),
                jnp.concatenate([f[1] for f in shards], 0),
                preferred_element_type=jnp.float32,
            ) + jnp.concatenate(near_sums, 0)
            for u, (sub, x) in enumerate(tiles):
                acc_ref[h, x, first + sub] = sums[u * tile : (u + 1) * tile]
        stat_ref[h] = stat


def attend_sides(pad, rows_in_band, q_all, *refs):
    far_sides, (acc_ref, stat_ref, out_ref), sides, sem = refs[:4], refs[4:7], refs[7:11], refs[11]
    copies = [
        pltpu.make_async_copy(source, target, sem.at[n])
        for n, (source, target) in enumerate(zip(far_sides, sides))
    ]
    for copy in copies:
        copy.start()
    heads, _, rows, tile, _ = acc_ref.shape
    key_rows = sides[0].shape[0] * rows_in_band
    lane = lax.broadcasted_iota(jnp.int32, (tile, tile), 1)
    near_rows = [[i for i in range(rows) if abs(i + pad - j) <= 1] for j in range(key_rows)]
    near_rows = {j: found for j, found in enumerate(near_rows) if found}
    for h, xq in [(h, xq) for xq in range(2) for h in range(heads)]:
        if h == 0:
            copies[2 * xq].wait()
            copies[2 * xq + 1].wait()
        stat = stat_ref[h]
        first, second = [at_head(a, h) for a in sides[2 * xq : 2 * xq + 2]]
        side = Band(first, second, rows_in_band, tile)
        mine = Band(None, at_head(q_all, h).at[xq], rows_in_band, tile, q_all.at[xq])
        pieces = {}
        for j, found in near_rows.items():
            qs = [mine.query(i // rows_in_band, i % rows_in_band) for i in found]
            s = scores(jnp.concatenate(qs, 0), side.key(j // rows_in_band, j % rows_in_band))
            for u, i in enumerate(found):
                pieces[i, j] = s[u * tile : (u + 1) * tile]
        shrinks, totals = {}, {}
        for i in range(rows):
            n = i * 2 + xq
            m_near = jnp.max(jnp.where(lane == n, stat, -jnp.inf), axis=1, keepdims=True)
            near = jnp.max(jnp.where(lane == n + tile // 2, stat, -jnp.inf), axis=1, keepdims=True)
            at = [j for j in near_rows if (i, j) in pieces]
            notes = mine.notes(i // rows_in_band, i % rows_in_band)
            masks = []
            for j in at:
                n = 6 + j - i - pad + 1
                masks.append(notes[n : n + 1] > 0)
            m, total, powers = softmax_terms([pieces[i, j] for j in at], masks, m_near)
            for u, j in enumerate(at):
                pieces[i, j] = powers[u]
            shrinks[i] = jnp.exp2((m_near - m) * LOG2_SCALE)
            totals[i] = total + near * shrinks[i]
        more = {}
        for j, found in near_rows.items():
            o = jnp.dot(
                jnp.concatenate([pieces[i, j] for i in found], 0),
                side.value(j // rows_in_band, j % rows_in_band),
                preferred_element_type=jnp.float32,
            )
            for u, i in enumerate(found):
                o_i = o[u * tile : (u + 1) * tile]
                more[i] = more[i] + o_i if i in more else o_i
        for i in range(rows):
            out = (acc_ref[h, xq, i] * shrinks[i] + more[i]) / totals[i]
            band, start = i // rows_in_band, i % rows_in_band * tile
            out_ref[xq, band, start : start + tile, h * HEAD_DIM : (h + 1) * HEAD_DIM] = out.astype(
                out_ref.dtype
            )


VMEM = pl.BlockSpec(memory_space=pltpu.VMEM)


def call(kernel, name, operands, out_shape, tiles, specs=None, scratch=()):
    flops = 4 * tiles * 128 * 128 * HEAD_DIM
    return pl.pallas_call(
        kernel,
        in_specs=specs or [VMEM] * len(operands),
        out_specs=jax.tree.map(lambda _: VMEM, out_shape),
        out_shape=out_shape,
        scratch_shapes=scratch,
        compiler_params=pltpu.CompilerParams(vmem_limit_bytes=40 * 1024 * 1024),
        cost_estimate=pl.CostEstimate(
            flops=flops, bytes_accessed=4 * 1024 * 1024, transcendentals=flops // 512
        ),
        name=name,
    )(*operands)


def start_pack(pieces, out_ref, sem):
    part, copies, at = out_ref.shape[-1], [], 0
    for n, (ref, first, end) in enumerate(pieces):
        for p in range(out_ref.shape[0]):
            copies.append(
                pltpu.make_async_copy(
                    ref.at[first:end, p * part : (p + 1) * part],
                    out_ref.at[p, at : at + end - first],
                    sem.at[n * out_ref.shape[0] + p],
                )
            )
        at += end - first
    for copy in copies:
        copy.start()
    return copies, at


def pack_first(cut, k_ref, v_ref, out_ref, sem):
    for copy in start_pack(((k_ref, 0, k_ref.shape[0]), (v_ref, 0, cut)), out_ref, sem)[0]:
        copy.wait()


def pack_second(cut, row_size, col_size, flags_ref, v_ref, q_ref, out_ref, sem):
    rows = q_ref.shape[0]
    copies, at = start_pack(((v_ref, cut, rows), (q_ref, 0, rows)), out_ref, sem)
    row_at, col_at = lax.axis_index("row"), lax.axis_index("col")
    tiles = flags_ref.shape[0]
    line = lax.broadcasted_iota(jnp.int32, (NOTE_ROWS, HEAD_DIM), 0)
    blocks = []
    inner = 1 - 2 * (col_at % 2)
    for t in range(tiles):
        notes = jnp.zeros(line.shape, jnp.float32)
        for kind, b in enumerate((0, inner, -inner)):
            for a in range(3):
                row, col = row_at * tiles + t + a - 1, col_at + b
                ok = (row >= 0) & (row < row_size * tiles) & (col >= 0) & (col < col_size)
                if kind or a != 1:
                    ok = ok & (flags_ref[t, 0, a * 3 + 1 + b] > 0)
                notes = jnp.where(line == kind * 3 + a, jnp.where(ok, 1.0, 0.0), notes)
        blocks.append(notes.astype(out_ref.dtype))
    for p in range(out_ref.shape[0]):
        for t, notes in enumerate(blocks):
            out_ref[p, at:, t * HEAD_DIM : (t + 1) * HEAD_DIM] = notes
    for copy in copies:
        copy.wait()


def packed(kernel, name, small, arrays, parts, rows):
    width = arrays[0].shape[1]
    return pl.pallas_call(
        kernel,
        in_specs=[pl.BlockSpec(memory_space=pltpu.SMEM)] * len(small)
        + [pl.BlockSpec(memory_space=pltpu.HBM)] * len(arrays),
        out_specs=VMEM,
        out_shape=jax.ShapeDtypeStruct(
            (parts, rows, width // parts), arrays[0].dtype
        ),
        scratch_shapes=[pltpu.SemaphoreType.DMA((len(arrays) * parts,))],
        compiler_params=pltpu.CompilerParams(vmem_limit_bytes=60 * 1024 * 1024),
        cost_estimate=pl.CostEstimate(flops=0, bytes_accessed=3 * 1024 * 1024, transcendentals=0),
        name=name,
    )(*small, *arrays)


def unpack(got_ref, out_ref):
    part = got_ref.shape[-1]
    for p in range(got_ref.shape[0]):
        out_ref[:, p * part : (p + 1) * part] = got_ref[p]


def moves(count, step):
    return [(i, i + step) for i in range(count) if 0 <= i + step < count]


def body(queries, fine_keys, fine_values, keep_flags, coarse_keys, coarse_values):
    rows_tiles, _, tile, width = queries.shape
    nrow, ncol = lax.axis_size("row"), lax.axis_size("col")
    band = min(4, nrow)
    planes = ncol // 2
    parts = band * 2
    part = width // parts
    rows = rows_tiles * tile
    row_at, col_at = lax.axis_index("row"), lax.axis_index("col")
    x_at, r_at = col_at % 2, row_at % band
    axes = ("row", "col")
    pad = 1 if nrow > band else 0
    groups = [
        [(g * band + r) * ncol + 2 * z + x for x in range(2) for r in range(band)]
        for g in range(nrow // band)
        for z in range(planes)
    ]

    def exchange(a):
        return lax.all_to_all(a, axes, 0, 0, axis_index_groups=groups, tiled=True)

    def coarse_of(x):
        at = (x * band + r_at) * part
        return jnp.stack(
            [lax.dynamic_slice_in_dim(c, at, part, 1) for c in (coarse_keys, coarse_values)]
        )

    here, away = coarse_of(x_at), coarse_of(1 - x_at)
    there = lax.ppermute(away, "col", [(c, c ^ 1) for c in range(ncol)])

    k, v, q = [a.reshape(rows, width) for a in (fine_keys, fine_values, queries)]
    cut = rows_tiles // 2 * tile
    sent = packed(functools.partial(pack_first, cut), "pack_first", (), (k, v), parts, rows + cut)
    sent, there = lax.optimization_barrier((sent, there))
    own = exchange(sent).reshape(2, band, rows + cut, part)
    pair = jnp.stack([here, there])
    far = [pair] + [
        lax.ppermute(pair, "col", [(c, (c + 2 * d) % ncol) for c in range(ncol)])
        for d in range(1, planes)
    ]

    def widen(a):
        line = a.reshape(band, 2, rows_tiles, tile, part)
        line = jnp.moveaxis(line, 1, 0).reshape(2, band * rows_tiles, tile, part)
        above = lax.ppermute(line[:, -1:], "row", moves(nrow, band))
        below = lax.ppermute(line[:, :1], "row", moves(nrow, -band))
        extra = [line[:, :1]] * ((-2) % rows_tiles)
        line = jnp.concatenate([above, line, below] + extra, 1)
        line = jnp.moveaxis(line.reshape(2, -1, rows_tiles, tile, part), 0, 1)
        return line.reshape(-1, 2 * rows, part)

    sent = packed(
        functools.partial(pack_second, cut, nrow, ncol),
        "pack_second",
        (keep_flags,),
        (v, q),
        parts,
        2 * rows - cut + NOTE_ROWS,
    )
    sent, far[1], far[2] = lax.optimization_barrier((sent, far[1], far[2]))
    q = exchange(sent).reshape(2, band, 2 * rows - cut + NOTE_ROWS, part)
    right_going, left_going = moves(ncol, 2), moves(ncol, -2)
    left, right = lax.ppermute(own[1], "col", right_going), lax.ppermute(own[0], "col", left_going)
    rest = q[:, :, : rows - cut]
    rest, far = lax.optimization_barrier((rest, far))
    left_rest = lax.ppermute(rest[1], "col", right_going)
    right_rest = lax.ppermute(rest[0], "col", left_going)
    own_rest = q
    if pad:

        def widened(first, second):
            both = widen(jnp.concatenate([first, second], 1))
            return both[:, : rows + cut], both[:, rows + cut :]

        left, left_rest = widened(left, left_rest)
        right, right_rest = widened(right, right_rest)
        wide = [widened(own[x], rest[x]) for x in range(2)]
        own, own_rest = jnp.stack([w[0] for w in wide]), jnp.stack([w[1] for w in wide])

    count, heads = band * rows_tiles, part // HEAD_DIM
    acc = jax.ShapeDtypeStruct((heads, 2, count, tile, HEAD_DIM), jnp.float32)
    stat = jax.ShapeDtypeStruct((heads, tile, tile), jnp.float32)
    acc, stat = call(
        functools.partial(attend_near, pad, rows_tiles),
        "attend_near",
        (q, own, own_rest, *far),
        (acc, stat),
        heads * 2 * count * (6 + 2 * planes),
        [VMEM] * 3 + [pl.BlockSpec(memory_space=pl.ANY)] * planes,
        [pltpu.VMEM(a.shape, a.dtype) for a in far] + [pltpu.SemaphoreType.DMA((planes,))],
    )
    sides = (left, left_rest, right, right_rest)
    out = call(
        functools.partial(attend_sides, pad, rows_tiles),
        "attend_sides",
        (q, *sides, acc, stat),
        jax.ShapeDtypeStruct((2, band, rows, part), queries.dtype),
        heads * 2 * count * 3,
        [VMEM] + [pl.BlockSpec(memory_space=pl.ANY)] * 4 + [VMEM] * 2,
        [pltpu.VMEM(a.shape, a.dtype) for a in sides] + [pltpu.SemaphoreType.DMA((4,))],
    )
    out = exchange(out.reshape(parts, rows, part))
    out = call(unpack, "unpack", (out,), jax.ShapeDtypeStruct((rows, width), queries.dtype), 0)
    return out.reshape(queries.shape)


def solution(mesh):
    placed = (
        P("row", "col", None, None),
        P("row", "col", None, None),
        P("row", "col", None, None),
        P("row", "col", None),
        P("col", None),
        P("col", None),
    )
    return jax.shard_map(
        body, mesh=mesh, in_specs=placed, out_specs=P("row", "col", None, None), check_vma=False
    )
```

```python
import functools

import jax
import jax.numpy as jnp
from jax import lax
from jax.experimental import pallas as pl
from jax.experimental.pallas import tpu as pltpu
from jax.sharding import PartitionSpec as P

HEADS = 16
HEAD_DIM = 128
LOG2_SCALE = HEAD_DIM ** (-0.5) * 1.4426950408889634


NT = (((1,), (1,)), ((), ()))
NOTE_ROWS = 16


def scores(a, b):
    return lax.dot_general(a, b, NT, preferred_element_type=jnp.float32)


def softmax_terms(pieces, masks, m):
    tiles = [s if ok is None else jnp.where(ok, s, -jnp.inf) for s, ok in zip(pieces, masks)]
    top = jnp.max(functools.reduce(jnp.maximum, tiles), axis=1, keepdims=True)
    m = top if m is None else jnp.maximum(m, top)
    powers, total = [], None
    for s in tiles:
        p = jnp.exp2((s - m) * LOG2_SCALE)
        total = p if total is None else total + p
        powers.append(p.astype(jnp.bfloat16))
    return m, jnp.sum(total, axis=1, keepdims=True), powers


def at_head(ref, h):
    return ref.at[..., h * HEAD_DIM : (h + 1) * HEAD_DIM]


class Band:
    def __init__(self, first, second, rows_in_band, tile, whole=None):
        self.first, self.second, self.rows, self.tile = first, second, rows_in_band, tile
        self.whole = whole
        self.cut = rows_in_band // 2

    def at(self, ref, band, n):
        return ref[band, n * self.tile : (n + 1) * self.tile]

    def key(self, band, sub):
        return self.at(self.first, band, sub)

    def value(self, band, sub):
        if sub < self.cut:
            return self.at(self.first, band, self.rows + sub)
        return self.at(self.second, band, sub - self.cut)

    def query(self, band, sub):
        return self.at(self.second, band, self.rows - self.cut + sub)

    def notes(self, band, sub):
        start, lane = (2 * self.rows - self.cut) * self.tile, sub * HEAD_DIM
        notes = self.whole[band, start : start + NOTE_ROWS, lane : lane + HEAD_DIM]
        return notes.astype(jnp.float32)


def attend_near(pad, rows_in_band, q_all, own_all, own_rest, *refs):
    planes = len(refs) // 2 - 1
    far_out, (acc_ref, stat_ref) = refs[:planes], refs[planes : planes + 2]
    far_all, sem = refs[planes + 2 : -1], refs[-1]
    copies = [
        pltpu.make_async_copy(source, target, sem.at[n])
        for n, (source, target) in enumerate(zip(far_out, far_all))
    ]
    for copy in copies:
        copy.start()
    heads, _, rows, tile, _ = acc_ref.shape
    key_rows = own_all.shape[1] * rows_in_band
    lane = lax.broadcasted_iota(jnp.int32, (tile, tile), 1)
    for h in range(heads):
        own, qs_of = [
            [
                Band(at_head(first, h).at[x], at_head(second, h).at[x], rows_in_band, tile, q_all.at[x])
                for x in range(2)
            ]
            for first, second in ((own_all, own_rest), (own_all, q_all))
        ]
        shards = [at_head(f, h).at[c] for f in far_all for c in range(2)]
        stat = jnp.zeros((tile, tile), jnp.float32)
        for first in range(0, rows, rows_in_band):
            band = first // rows_in_band
            tiles = [(sub, x) for sub in range(rows_in_band) for x in range(2)]
            qs = [qs_of[x].query(band, sub) for sub, x in tiles]
            windows, nears = [], []
            for sub in range(rows_in_band):
                at = [(a, first + sub + pad + a - 1) for a in range(3)]
                at = [(a, j // rows_in_band, j % rows_in_band) for a, j in at if 0 <= j < key_rows]
                window = [(a, kb, ks, x) for a, kb, ks in at for x in range(2)]
                windows.append(window)
                nears.append(
                    scores(
                        jnp.concatenate(qs[2 * sub : 2 * sub + 2], 0),
                        jnp.concatenate([own[x].key(kb, ks) for _, kb, ks, x in window], 0),
                    )
                )
            if h == 0 and first == 0:
                for copy in copies:
                    copy.wait()
            far = scores(jnp.concatenate(qs, 0), jnp.concatenate([f[0] for f in shards], 0))
            far_powers, near_sums = [], []
            for sub in range(rows_in_band):
                i, window, near = first + sub, windows[sub], nears[sub]
                near_powers = []
                for xq in range(2):
                    mine = slice((2 * sub + xq) * tile, (2 * sub + xq + 1) * tile)
                    pieces = [far[mine, n * tile : (n + 1) * tile] for n in range(len(shards))]
                    mine = slice(xq * tile, (xq + 1) * tile)
                    pieces += [near[mine, n * tile : (n + 1) * tile] for n in range(len(window))]
                    notes = qs_of[xq].notes(band, sub)
                    masks = [None] * len(shards)
                    for a, _, _, x in window:
                        n = (x ^ xq) * 3 + a
                        masks.append(None if x == xq and a == 1 else notes[n : n + 1] > 0)
                    m, total, powers = softmax_terms(pieces, masks, None)
                    far_powers.append(jnp.concatenate(powers[: len(shards)], 1))
                    near_powers.append(jnp.concatenate(powers[len(shards) :], 1))
                    n = i * 2 + xq
                    stat = jnp.where(lane == n, m, jnp.where(lane == n + tile // 2, total, stat))
                near_sums.append(
                    jnp.dot(
                        jnp.concatenate(near_powers, 0),
                        jnp.concatenate([own[x].value(kb, ks) for _, kb, ks, x in window], 0),
                        preferred_element_type=jnp.float32,
                    )
                )
            sums = jnp.dot(
                jnp.concatenate(far_powers, 0),
                jnp.concatenate([f[1] for f in shards], 0),
                preferred_element_type=jnp.float32,
            ) + jnp.concatenate(near_sums, 0)
            for u, (sub, x) in enumerate(tiles):
                acc_ref[h, x, first + sub] = sums[u * tile : (u + 1) * tile]
        stat_ref[h] = stat


def attend_sides(pad, rows_in_band, q_all, *refs):
    far_sides, (acc_ref, stat_ref, out_ref), sides, sem = refs[:4], refs[4:7], refs[7:11], refs[11]
    copies = [
        pltpu.make_async_copy(source, target, sem.at[n])
        for n, (source, target) in enumerate(zip(far_sides, sides))
    ]
    for copy in copies:
        copy.start()
    heads, _, rows, tile, _ = acc_ref.shape
    key_rows = sides[0].shape[0] * rows_in_band
    lane = lax.broadcasted_iota(jnp.int32, (tile, tile), 1)
    near_rows = [[i for i in range(rows) if abs(i + pad - j) <= 1] for j in range(key_rows)]
    near_rows = {j: found for j, found in enumerate(near_rows) if found}
    for h, xq in [(h, xq) for xq in range(2) for h in range(heads)]:
        if h == 0:
            copies[2 * xq].wait()
            copies[2 * xq + 1].wait()
        stat = stat_ref[h]
        first, second = [at_head(a, h) for a in sides[2 * xq : 2 * xq + 2]]
        side = Band(first, second, rows_in_band, tile)
        mine = Band(None, at_head(q_all, h).at[xq], rows_in_band, tile, q_all.at[xq])
        pieces = {}
        for j, found in near_rows.items():
            qs = [mine.query(i // rows_in_band, i % rows_in_band) for i in found]
            s = scores(jnp.concatenate(qs, 0), side.key(j // rows_in_band, j % rows_in_band))
            for u, i in enumerate(found):
                pieces[i, j] = s[u * tile : (u + 1) * tile]
        shrinks, totals = {}, {}
        for i in range(rows):
            n = i * 2 + xq
            m_near = jnp.max(jnp.where(lane == n, stat, -jnp.inf), axis=1, keepdims=True)
            near = jnp.max(jnp.where(lane == n + tile // 2, stat, -jnp.inf), axis=1, keepdims=True)
            at = [j for j in near_rows if (i, j) in pieces]
            notes = mine.notes(i // rows_in_band, i % rows_in_band)
            masks = []
            for j in at:
                n = 6 + j - i - pad + 1
                masks.append(notes[n : n + 1] > 0)
            m, total, powers = softmax_terms([pieces[i, j] for j in at], masks, m_near)
            for u, j in enumerate(at):
                pieces[i, j] = powers[u]
            shrinks[i] = jnp.exp2((m_near - m) * LOG2_SCALE)
            totals[i] = total + near * shrinks[i]
        more = {}
        for j, found in near_rows.items():
            o = jnp.dot(
                jnp.concatenate([pieces[i, j] for i in found], 0),
                side.value(j // rows_in_band, j % rows_in_band),
                preferred_element_type=jnp.float32,
            )
            for u, i in enumerate(found):
                o_i = o[u * tile : (u + 1) * tile]
                more[i] = more[i] + o_i if i in more else o_i
        for i in range(rows):
            out = (acc_ref[h, xq, i] * shrinks[i] + more[i]) / totals[i]
            band, start = i // rows_in_band, i % rows_in_band * tile
            out_ref[xq, band, start : start + tile, h * HEAD_DIM : (h + 1) * HEAD_DIM] = out.astype(
                out_ref.dtype
            )


VMEM = pl.BlockSpec(memory_space=pltpu.VMEM)


def call(kernel, name, operands, out_shape, tiles, specs=None, scratch=()):
    flops = 4 * tiles * 128 * 128 * HEAD_DIM
    return pl.pallas_call(
        kernel,
        in_specs=specs or [VMEM] * len(operands),
        out_specs=jax.tree.map(lambda _: VMEM, out_shape),
        out_shape=out_shape,
        scratch_shapes=scratch,
        compiler_params=pltpu.CompilerParams(vmem_limit_bytes=40 * 1024 * 1024),
        cost_estimate=pl.CostEstimate(
            flops=flops, bytes_accessed=4 * 1024 * 1024, transcendentals=flops // 512
        ),
        name=name,
    )(*operands)


def start_pack(pieces, out_ref, sem):
    part, copies, at = out_ref.shape[-1], [], 0
    base = pl.program_id(0) * out_ref.shape[0]
    for n, (ref, first, end) in enumerate(pieces):
        for p in range(out_ref.shape[0]):
            copies.append(
                pltpu.make_async_copy(
                    ref.at[first:end, pl.ds(pl.multiple_of((base + p) * part, part), part)],
                    out_ref.at[p, at : at + end - first],
                    sem.at[n * out_ref.shape[0] + p],
                )
            )
        at += end - first
    for copy in copies:
        copy.start()
    return copies, at


def pack_first(cut, k_ref, v_ref, out_ref, sem):
    for copy in start_pack(((k_ref, 0, k_ref.shape[0]), (v_ref, 0, cut)), out_ref, sem)[0]:
        copy.wait()


def pack_second(cut, row_size, col_size, flags_ref, v_ref, q_ref, out_ref, sem):
    rows = q_ref.shape[0]
    copies, at = start_pack(((v_ref, cut, rows), (q_ref, 0, rows)), out_ref, sem)
    row_at, col_at = lax.axis_index("row"), lax.axis_index("col")
    tiles = flags_ref.shape[0]
    line = lax.broadcasted_iota(jnp.int32, (NOTE_ROWS, HEAD_DIM), 0)
    blocks = []
    inner = 1 - 2 * (col_at % 2)
    for t in range(tiles):
        notes = jnp.zeros(line.shape, jnp.float32)
        for kind, b in enumerate((0, inner, -inner)):
            for a in range(3):
                row, col = row_at * tiles + t + a - 1, col_at + b
                ok = (row >= 0) & (row < row_size * tiles) & (col >= 0) & (col < col_size)
                if kind or a != 1:
                    ok = ok & (flags_ref[t, 0, a * 3 + 1 + b] > 0)
                notes = jnp.where(line == kind * 3 + a, jnp.where(ok, 1.0, 0.0), notes)
        blocks.append(notes.astype(out_ref.dtype))
    for p in range(out_ref.shape[0]):
        for t, notes in enumerate(blocks):
            out_ref[p, at:, t * HEAD_DIM : (t + 1) * HEAD_DIM] = notes
    for copy in copies:
        copy.wait()


def packed(kernel, name, small, arrays, parts, rows):
    width = arrays[0].shape[1]
    return pl.pallas_call(
        kernel,
        in_specs=[pl.BlockSpec(memory_space=pltpu.SMEM)] * len(small)
        + [pl.BlockSpec(memory_space=pltpu.HBM)] * len(arrays),
        grid=(2,),
        out_specs=pl.BlockSpec((parts // 2, rows, width // parts), lambda s: (s, 0, 0)),
        out_shape=jax.ShapeDtypeStruct(
            (parts, rows, width // parts), arrays[0].dtype
        ),
        scratch_shapes=[pltpu.SemaphoreType.DMA((len(arrays) * parts,))],
        compiler_params=pltpu.CompilerParams(vmem_limit_bytes=60 * 1024 * 1024),
        cost_estimate=pl.CostEstimate(flops=0, bytes_accessed=3 * 1024 * 1024, transcendentals=0),
        name=name,
    )(*small, *arrays)


def unpack(got_ref, out_ref):
    part = got_ref.shape[-1]
    for p in range(got_ref.shape[0]):
        out_ref[:, p * part : (p + 1) * part] = got_ref[p]


def moves(count, step):
    return [(i, i + step) for i in range(count) if 0 <= i + step < count]


def body(queries, fine_keys, fine_values, keep_flags, coarse_keys, coarse_values):
    rows_tiles, _, tile, width = queries.shape
    nrow, ncol = lax.axis_size("row"), lax.axis_size("col")
    band = min(4, nrow)
    planes = ncol // 2
    parts = band * 2
    part = width // parts
    rows = rows_tiles * tile
    row_at, col_at = lax.axis_index("row"), lax.axis_index("col")
    x_at, r_at = col_at % 2, row_at % band
    axes = ("row", "col")
    pad = 1 if nrow > band else 0
    groups = [
        [(g * band + r) * ncol + 2 * z + x for x in range(2) for r in range(band)]
        for g in range(nrow // band)
        for z in range(planes)
    ]

    def exchange(a):
        return lax.all_to_all(a, axes, 0, 0, axis_index_groups=groups, tiled=True)

    def coarse_of(x):
        at = (x * band + r_at) * part
        return jnp.stack(
            [lax.dynamic_slice_in_dim(c, at, part, 1) for c in (coarse_keys, coarse_values)]
        )

    here, away = coarse_of(x_at), coarse_of(1 - x_at)
    there = lax.ppermute(away, "col", [(c, c ^ 1) for c in range(ncol)])

    k, v, q = [a.reshape(rows, width) for a in (fine_keys, fine_values, queries)]
    cut = rows_tiles // 2 * tile
    sent = packed(functools.partial(pack_first, cut), "pack_first", (), (k, v), parts, rows + cut)
    sent, there = lax.optimization_barrier((sent, there))
    own = exchange(sent).reshape(2, band, rows + cut, part)
    pair = jnp.stack([here, there])
    far = [pair] + [
        lax.ppermute(pair, "col", [(c, (c + 2 * d) % ncol) for c in range(ncol)])
        for d in range(1, planes)
    ]

    def widen(a):
        line = a.reshape(band, 2, rows_tiles, tile, part)
        line = jnp.moveaxis(line, 1, 0).reshape(2, band * rows_tiles, tile, part)
        above = lax.ppermute(line[:, -1:], "row", moves(nrow, band))
        below = lax.ppermute(line[:, :1], "row", moves(nrow, -band))
        extra = [line[:, :1]] * ((-2) % rows_tiles)
        line = jnp.concatenate([above, line, below] + extra, 1)
        line = jnp.moveaxis(line.reshape(2, -1, rows_tiles, tile, part), 0, 1)
        return line.reshape(-1, 2 * rows, part)

    sent = packed(
        functools.partial(pack_second, cut, nrow, ncol),
        "pack_second",
        (keep_flags,),
        (v, q),
        parts,
        2 * rows - cut + NOTE_ROWS,
    )
    sent, far[1], far[2] = lax.optimization_barrier((sent, far[1], far[2]))
    q = exchange(sent).reshape(2, band, 2 * rows - cut + NOTE_ROWS, part)
    right_going, left_going = moves(ncol, 2), moves(ncol, -2)
    left, right = lax.ppermute(own[1], "col", right_going), lax.ppermute(own[0], "col", left_going)
    rest = q[:, :, : rows - cut]
    rest, far = lax.optimization_barrier((rest, far))
    left_rest = lax.ppermute(rest[1], "col", right_going)
    right_rest = lax.ppermute(rest[0], "col", left_going)
    own_rest = q
    if pad:

        def widened(first, second):
            both = widen(jnp.concatenate([first, second], 1))
            return both[:, : rows + cut], both[:, rows + cut :]

        left, left_rest = widened(left, left_rest)
        right, right_rest = widened(right, right_rest)
        wide = [widened(own[x], rest[x]) for x in range(2)]
        own, own_rest = jnp.stack([w[0] for w in wide]), jnp.stack([w[1] for w in wide])

    count, heads = band * rows_tiles, part // HEAD_DIM
    acc = jax.ShapeDtypeStruct((heads, 2, count, tile, HEAD_DIM), jnp.float32)
    stat = jax.ShapeDtypeStruct((heads, tile, tile), jnp.float32)
    acc, stat = call(
        functools.partial(attend_near, pad, rows_tiles),
        "attend_near",
        (q, own, own_rest, *far),
        (acc, stat),
        heads * 2 * count * (6 + 2 * planes),
        [VMEM] * 3 + [pl.BlockSpec(memory_space=pl.ANY)] * planes,
        [pltpu.VMEM(a.shape, a.dtype) for a in far] + [pltpu.SemaphoreType.DMA((planes,))],
    )
    sides = (left, left_rest, right, right_rest)
    out = call(
        functools.partial(attend_sides, pad, rows_tiles),
        "attend_sides",
        (q, *sides, acc, stat),
        jax.ShapeDtypeStruct((2, band, rows, part), queries.dtype),
        heads * 2 * count * 3,
        [VMEM] + [pl.BlockSpec(memory_space=pl.ANY)] * 4 + [VMEM] * 2,
        [pltpu.VMEM(a.shape, a.dtype) for a in sides] + [pltpu.SemaphoreType.DMA((4,))],
    )
    out = exchange(out.reshape(parts, rows, part))
    out = call(unpack, "unpack", (out,), jax.ShapeDtypeStruct((rows, width), queries.dtype), 0)
    return out.reshape(queries.shape)


def solution(mesh):
    placed = (
        P("row", "col", None, None),
        P("row", "col", None, None),
        P("row", "col", None, None),
        P("row", "col", None),
        P("col", None),
        P("col", None),
    )
    return jax.shard_map(
        body, mesh=mesh, in_specs=placed, out_specs=P("row", "col", None, None), check_vma=False
    )
```
